32 devices in a mesh: wide: 8 (over z, y), narrow: 4 (over x, core).
Axes of the slice: x: 2, y: 2, z: 4, core: 2. Of those that a mesh axis runs over, the one named last changes fastest.
Arguments:
- occupied: bfloat16 [64, 64, 4096], P('wide', 'narrow'), may hold values from -6 to 6
- empty: bfloat16 [128, 64, 4096], P('wide', 'narrow'), may hold values from -6 to 6
- pair_occ: int32 [256], P('wide'), may hold values from 0 to 7
- pair_emp: int32 [256], P('wide'), may hold values from 0 to 15
- pair_level: int32 [256], replicated, may hold values from 0 to 63
- denominators: float32 [64, 8], replicated, may hold values from 0.02 to 0.2
- trial: bfloat16 [131072, 512], P(('wide', 'narrow')), may hold values from -0.015625 to 0.015625
Outputs:
- response: bfloat16 [8, 131072, 512], P(None, ('wide', 'narrow'))
The draws below stay inside these ranges and needn't reach their ends.
Inputs may be any that keep to these rules, and one draw needn't show every extreme that they name: Pair p uses occupied band (p // 32) * 8 + pair_occ[p]. Pair p uses empty band (p // 32) * 16 + pair_emp[p].
All inputs are finite; a program needn't handle non-finite values.
Results may differ from the reference program's by a relative error of at most 0.012.
Values may be sent and summed in bfloat16 or wider, within the bound.
No kernel may reach another device: no remote copies, remote signals or barrier semaphores. Data moves between devices by JAX's collectives and lax.ppermute only.
A program may use at most 128 MiB of HBM per device.

```python
import math
import jax
import jax.numpy as jnp
from jax import lax

GRID = 64
K = 512
NW = 8
NTAB = 64
OCC_DEV = 8
EMP_DEV = 16
P_DEV = 32
N_OCC = 64
N_EMP = 128
PAIRS = 256
COLS = 131072
N_WIDE = 8
N_NARROW = 4


def touch_ends(result, rng, least, largest):
    longest = result.shape.index(max(result.shape))
    spots = []
    for shift in (0, 1):
        where = [jax.random.randint(jax.random.fold_in(rng, axis), (), 0, length) for axis, length in enumerate(result.shape)]
        where[longest] = (where[longest] + shift) % result.shape[longest]
        spots.append(tuple(where))
    return result.at[spots[0]].set(least).at[spots[1]].set(largest)


def block_scale(stream_key, dims, shards, least, high):
    level = 1.0
    for axis_at, parts in shards:
        steps = jax.random.uniform(jax.random.fold_in(jax.random.fold_in(stream_key, 6), axis_at), (parts,), jnp.float32, least / len(shards), high / len(shards))
        level = level * jnp.repeat(jnp.exp(steps), dims[axis_at] // parts).reshape((-1,) + (1,) * (len(dims) - 1 - axis_at))
    return level


def normal_values(rng, shape, width, most, cuts=(), held_as=jnp.bfloat16):
    array = width * jax.random.normal(rng, shape, jnp.float32)
    if cuts:
        array = array * block_scale(rng, shape, cuts, -0.22, 0.18)
    return jnp.clip(array, -most, most).astype(held_as)


def setup_inputs(seed: int = 0) -> dict:
    key_list = jax.random.split(jax.random.key(seed), 8)
    return {
        "occupied": normal_values(key_list[0], (N_OCC, GRID, GRID * GRID), 1.0, 6.0, ((0, 8), (1, 4))),
        "empty": normal_values(key_list[1], (N_EMP, GRID, GRID * GRID), 1.0, 6.0, ((0, 8), (1, 4))),
        "pair_occ": touch_ends(jax.random.randint(key_list[2], (PAIRS,), 0, OCC_DEV), jax.random.fold_in(key_list[2], 1), 0, OCC_DEV - 1).astype(jnp.int32),
        "pair_emp": touch_ends(jax.random.randint(key_list[3], (PAIRS,), 0, EMP_DEV), jax.random.fold_in(key_list[3], 1), 0, EMP_DEV - 1).astype(jnp.int32),
        "pair_level": touch_ends(jax.random.randint(key_list[4], (PAIRS,), 0, NTAB), jax.random.fold_in(key_list[4], 1), 0, NTAB - 1).astype(jnp.int32),
        "denominators": jnp.clip(jnp.exp(jax.random.uniform(key_list[5], (NTAB, NW), jnp.float32, math.log(0.02), math.log(0.2))), 0.02, 0.2),
        "trial": normal_values(key_list[6], (COLS, K), COLS ** -0.5, 0.015625, ((0, 32),)),
    }


def tables(grid_size):
    positions = jnp.arange(grid_size, dtype=jnp.int32)
    half_range = jnp.arange(grid_size // 2, dtype=jnp.int32)
    scaling = 1.0 / math.sqrt(grid_size)
    step_angle = 2.0 * math.pi / grid_size
    z_angles = (positions[:, None] * half_range[None, :] % grid_size).astype(jnp.float32) * step_angle
    z_table = jnp.stack([jnp.cos(z_angles), -jnp.sin(z_angles)], -1).reshape(grid_size, grid_size) * scaling
    signed = jnp.where(half_range < grid_size // 4, half_range, half_range - grid_size // 2)
    y_angles = (signed[:, None] * positions[None, :] % grid_size).astype(jnp.float32) * step_angle
    y_table = jnp.stack([jnp.cos(y_angles), jnp.sin(y_angles)]) * scaling
    x_angles = (positions[:, None] * positions[None, :] % grid_size).astype(jnp.float32) * step_angle
    x_table = jnp.stack([jnp.cos(x_angles), jnp.sin(x_angles)]) * scaling
    return (z_table.astype(jnp.bfloat16), y_table.astype(jnp.bfloat16), x_table.astype(jnp.bfloat16))

def combine_parts(stacked):
    full_shape = stacked.shape[1:]
    halves = stacked.reshape(stacked.shape[:-1] + (stacked.shape[-1] // 2, 2))
    real_part = halves[0, ..., 0] + halves[1, ..., 1]
    imag_part = halves[0, ..., 1] - halves[1, ..., 0]
    return jnp.stack([real_part, imag_part], -1).reshape(full_shape)

def arrange(values, grid_size):
    values = values.reshape(grid_size, grid_size // 2, N_NARROW, grid_size // N_NARROW)
    values = jnp.transpose(values, (2, 0, 1, 3)).reshape(N_NARROW, N_WIDE, -1)
    return jnp.transpose(values, (1, 0, 2)).reshape(-1)

def coulomb_vector(grid_size):
    freq_x = jnp.arange(grid_size, dtype=jnp.int32)
    freq_x = jnp.where(freq_x < grid_size // 2, freq_x, freq_x - grid_size)
    freq_y = jnp.arange(grid_size // 2, dtype=jnp.int32)
    freq_y = jnp.where(freq_y < grid_size // 4, freq_y, freq_y - grid_size // 2)
    freq_z = jnp.arange(grid_size, dtype=jnp.int32) // 2
    squared = (freq_x[:, None, None] ** 2 + freq_y[None, :, None] ** 2 + freq_z[None, None, :] ** 2).astype(jnp.float32)
    quarter = float(grid_size // 4)
    return arrange(1.0 / jnp.sqrt(1.0 + squared / (quarter * quarter)), grid_size)

def pair_row(products, z_table, y_table, x_table):
    grid_size = products.shape[0]
    along_z = jnp.einsum('xyz,za->xya', products.astype(jnp.float32), z_table.astype(jnp.float32)).astype(jnp.bfloat16)
    along_y = combine_parts(jnp.einsum('sky,xyq->sxkq', y_table.astype(jnp.float32), along_z.astype(jnp.float32))).astype(jnp.bfloat16)
    along_x = combine_parts(jnp.einsum('skx,xyq->skyq', x_table.astype(jnp.float32), along_y.astype(jnp.float32))).astype(jnp.bfloat16)
    return arrange(along_x, grid_size)

def reference(occupied, empty, pair_occ, pair_emp, pair_level, denominators, trial):
    z_table, y_table, x_table = tables(GRID)
    pair_index = jnp.arange(pair_occ.shape[0], dtype=jnp.int32)
    occ_index = pair_index // P_DEV * OCC_DEV + pair_occ
    emp_index = pair_index // P_DEV * EMP_DEV + pair_emp

    def pair_wave(indices):
        products = (occupied[indices[0]].astype(jnp.float32) * empty[indices[1]].astype(jnp.float32)).astype(jnp.bfloat16)
        return pair_row(products.reshape(GRID, GRID, GRID), z_table, y_table, x_table)
    pair_waves = lax.map(pair_wave, jnp.stack([occ_index, emp_index], 1))
    coulomb = coulomb_vector(GRID)
    scaled = (coulomb[:, None] * trial.astype(jnp.float32)).astype(jnp.bfloat16)
    projections = jnp.dot(pair_waves, scaled, preferred_element_type=jnp.float32)
    weights = denominators[pair_level]
    weighted = (jnp.transpose(weights)[:, :, None] * projections[None]).astype(jnp.bfloat16)
    total_cols = pair_waves.shape[1]
    block_width = math.gcd(total_cols, 4096)
    weighted_wide = weighted.astype(jnp.float32)

    def column_block(block_index):
        pair_block = lax.dynamic_slice_in_dim(pair_waves, block_index * block_width, block_width, 1)
        product_sum = jnp.einsum('pc,wpk->wck', pair_block.astype(jnp.float32), weighted_wide)
        coulomb_block = lax.dynamic_slice_in_dim(coulomb, block_index * block_width, block_width, 0)
        return (product_sum * coulomb_block[None, :, None]).astype(jnp.bfloat16)
    blocks = lax.map(column_block, jnp.arange(total_cols // block_width, dtype=jnp.int32))
    return jnp.transpose(blocks, (1, 0, 2, 3)).reshape(NW, total_cols, trial.shape[1])
```

```python
import functools
import math

import jax
import jax.numpy as jnp
import numpy as np
from jax import lax
from jax.experimental import pallas as pl
from jax.experimental.pallas import tpu as pltpu
from jax.sharding import PartitionSpec as P

GROUP = 16
LANES = 128
SPLITS = ((1, 1), (1,))
PERMUTE_MOST = 8
VMEM = 56 * 1024 * 1024
F32 = jnp.float32
BF16 = jnp.bfloat16


def rounded(values):
    return np.asarray(values, np.float32).astype(jnp.bfloat16)


def tables(grid, slabs):
    scaling = np.float32(1.0 / math.sqrt(grid))
    step = np.float32(2.0 * math.pi / grid)
    at = np.arange(grid)
    half = np.arange(grid // 2)

    def cos_sin(a, b):
        angle = (a[:, None] * b[None, :] % grid).astype(np.float32) * step
        return (
            rounded(np.cos(angle) * scaling).astype(np.float32),
            rounded(np.sin(angle) * scaling).astype(np.float32),
        )

    planes = grid // slabs
    depth = grid // 2 // slabs
    channels = 2 * depth
    group = LANES // channels
    zc, zs = cos_sin(at, half)
    ztab = np.stack([zc, -zs], -1).reshape(grid, slabs, channels)
    zmat = np.einsum("ab,znq->aznbq", np.eye(group, dtype=np.float32), ztab)
    zmat = zmat.reshape(group * grid, slabs * group * channels)
    signed = np.where(half < grid // 4, half, half - grid // 2)
    yc, ys = cos_sin(signed, at)
    mix = np.zeros((grid, 2, grid // 2, 2), np.float32)
    mix[:, 0, :, 0] = yc.T
    mix[:, 1, :, 0] = ys.T
    mix[:, 0, :, 1] = -ys.T
    mix[:, 1, :, 1] = yc.T
    ymat = np.einsum("yajb,dk->ydajkb", mix, np.eye(depth, dtype=np.float32))
    ymat = ymat.reshape(grid * channels, grid // 2 * channels)
    xc, xs = cos_sin(at, at)
    xtab = np.stack([xc, xs]).reshape(2, grid, slabs, planes)
    xmat = np.einsum("hksx,pr->skphrx", xtab, np.eye(8, dtype=np.float32))
    xmat = xmat.reshape(slabs, grid * 8, 2 * 8 * planes)
    swap = np.zeros((2 * LANES, 2 * LANES), np.float32)
    even = np.arange(0, 2 * LANES, 2)
    swap[even + 1, even] = 1.0
    swap[even, even + 1] = -1.0
    return rounded(zmat), rounded(ymat), rounded(xmat), rounded(swap)


def front_kernel(start, slabs, widths, occ_at, emp_at, places, occ, emp, zmat, ymat, *rest):
    outs, (prod, lines) = rest[:-2], rest[-2:]
    planes = occ.shape[1]
    width = zmat.shape[0]
    steps = occ.shape[2] // width
    for p in range(GROUP):
        o, e = occ_at[start + p], emp_at[start + p]
        row = (occ[o].astype(F32) * emp[e].astype(F32)).astype(BF16)
        for g in range(steps):
            prod[g, p * planes : (p + 1) * planes, :] = row[:, g * width : (g + 1) * width]
    for g in range(steps):
        along = jnp.dot(prod[g], zmat[...], preferred_element_type=F32).astype(BF16)
        for n in range(slabs):
            lines[n, :, g * LANES : (g + 1) * LANES] = along[:, n * LANES : (n + 1) * LANES]
    for s in range(slabs):
        along = jnp.dot(lines[places[s]], ymat[...], preferred_element_type=F32).astype(BF16)
        first = 0
        for h, wide in enumerate(widths):
            outs[h * slabs + s][...] = along[:, first : first + wide]
            first += wide


def front(start, slabs, widths, occ_at, emp_at, places, occ, emp, zmat, ymat):
    rows = GROUP * occ.shape[1]
    width = zmat.shape[0]
    steps = occ.shape[2] // width
    smem = pl.BlockSpec(memory_space=pltpu.SMEM)
    vmem = pl.BlockSpec(memory_space=pltpu.VMEM)
    flops = 2 * rows * (steps * width * zmat.shape[1] + slabs * ymat.shape[0] * ymat.shape[1])
    outs = pl.pallas_call(
        functools.partial(front_kernel, start, slabs, widths),
        out_shape=[jax.ShapeDtypeStruct((rows, w), BF16) for w in widths for _ in range(slabs)],
        in_specs=[smem] * 3 + [vmem] * 4,
        out_specs=[vmem] * (len(widths) * slabs),
        scratch_shapes=[
            pltpu.VMEM((steps, rows, width), BF16),
            pltpu.VMEM((slabs, rows, ymat.shape[0]), BF16),
        ],
        compiler_params=pltpu.CompilerParams(vmem_limit_bytes=VMEM),
        cost_estimate=pl.CostEstimate(
            flops=flops, bytes_accessed=2 * (occ.size + emp.size), transcendentals=0
        ),
        name="front",
    )(occ_at, emp_at, places, occ, emp, zmat, ymat)
    return [outs[h * slabs : (h + 1) * slabs] for h in range(len(widths))]


def across_kernel(slabs, blocks, first, grid, places, *rest):
    parts, (xmat, swap), outs, whole = (
        rest[:slabs],
        rest[slabs : slabs + 2],
        rest[slabs + 2 : -1],
        rest[-1],
    )
    wide = parts[0].shape[1]
    planes = parts[0].shape[0] // GROUP
    half = grid // 2
    channels = 2 * (half // slabs)
    lane = first + lax.broadcasted_iota(jnp.int32, (grid, wide), 1)
    kx = lax.broadcasted_iota(jnp.int32, (grid, wide), 0)
    kx = jnp.where(kx < half, kx, kx - grid)
    ky = lane // channels
    ky = jnp.where(ky < half // 2, ky, ky - half)
    kz = places[0] * (channels // 2) + lane % channels // 2
    squared = (kx * kx + ky * ky + kz * kz).astype(F32)
    quarter = float(grid // 4)
    coulomb = (1.0 / jnp.sqrt(1.0 + squared / (quarter * quarter)))[:, None, :]
    left = jnp.concatenate([xmat[places[s]] for s in range(slabs)], axis=1)
    found = []
    for m in range(GROUP // 8):
        right = []
        for s in range(slabs):
            plain = parts[s][m * 8 * planes : (m + 1) * 8 * planes, :]
            right.append(plain)
            turned = [
                jnp.dot(plain[:, c : c + 2 * LANES], swap[...], preferred_element_type=F32)
                for c in range(0, wide, 2 * LANES)
            ]
            right.append(jnp.concatenate(turned, axis=1).astype(BF16))
        right = jnp.concatenate(right, axis=0)
        total = jnp.dot(left, right, preferred_element_type=F32)
        found.append(total.reshape(grid, 8, wide) * coulomb)
    found = jnp.concatenate(found, axis=1).astype(BF16)
    whole[...] = found.reshape(whole.shape)
    for s in range(blocks):
        outs[s][...] = whole[places[slabs + s]]


def across(slabs, blocks, first, grid, places, parts, xmat, swap):
    rows, wide = parts[0].shape
    tall = grid // blocks * GROUP
    smem = pl.BlockSpec(memory_space=pltpu.SMEM)
    vmem = pl.BlockSpec(memory_space=pltpu.VMEM)
    flops = 2 * GROUP // 8 * xmat.shape[1] * xmat.shape[2] * slabs * wide
    return pl.pallas_call(
        functools.partial(across_kernel, slabs, blocks, first, grid),
        out_shape=[jax.ShapeDtypeStruct((tall, wide), BF16)] * blocks,
        in_specs=[smem] + [vmem] * (slabs + 2),
        out_specs=[vmem] * blocks,
        scratch_shapes=[pltpu.VMEM((blocks, tall, wide), BF16)],
        compiler_params=pltpu.CompilerParams(vmem_limit_bytes=VMEM),
        cost_estimate=pl.CostEstimate(
            flops=flops, bytes_accessed=4 * slabs * rows * wide, transcendentals=0
        ),
        name="across",
    )(places, *parts, xmat, swap)


def project_kernel(blocks, slabs, widths, places, trial, *rest):
    parts, (shares, turned) = rest[:-2], rest[-2:]
    count = blocks * len(widths)
    parts = parts[:count]
    lanes = sum(widths)
    heights = parts[0].shape[0] // GROUP
    total = jnp.zeros((blocks * GROUP, trial.shape[1]), F32)
    for x in range(heights):
        first = x * lanes
        for h, wide in enumerate(widths):
            left = jnp.concatenate(
                [parts[h * blocks + s][x * GROUP : (x + 1) * GROUP, :] for s in range(blocks)], axis=0
            )
            total += jnp.dot(left, trial[first : first + wide, :], preferred_element_type=F32)
            turned[first : first + wide, :] = left.T
            first += wide
    step = trial.shape[1] // slabs
    for s in range(blocks):
        for n in range(slabs):
            shares[places[slabs + s] * slabs + n] = total[
                s * GROUP : (s + 1) * GROUP, n * step : (n + 1) * step
            ].astype(shares.dtype)


def project(blocks, slabs, widths, places, trial, parts):
    columns, vectors = trial.shape
    pairs = blocks * GROUP
    smem = pl.BlockSpec(memory_space=pltpu.SMEM)
    vmem = pl.BlockSpec(memory_space=pltpu.VMEM)
    return pl.pallas_call(
        functools.partial(project_kernel, blocks, slabs, widths),
        out_shape=[
            jax.ShapeDtypeStruct((blocks * slabs, GROUP, vectors // slabs), BF16),
            jax.ShapeDtypeStruct((columns, pairs), BF16),
        ],
        in_specs=[smem] + [vmem] * (1 + len(parts)),
        out_specs=[vmem] * 2,
        compiler_params=pltpu.CompilerParams(vmem_limit_bytes=VMEM),
        cost_estimate=pl.CostEstimate(
            flops=2 * pairs * columns * vectors,
            bytes_accessed=2 * columns * (vectors + 2 * pairs),
            transcendentals=0,
        ),
        name="project",
    )(places, trial, *parts)


def respond_kernel(blocks, slabs, groups, freqs, places, *rest):
    shares = rest[:groups]
    weights = rest[groups : 2 * groups]
    turned = rest[2 * groups : 3 * groups]
    out, weighted = rest[3 * groups :]
    vectors = out.shape[2]
    step = vectors // slabs

    @pl.when(pl.program_id(0) == 0)
    def _():
        for g in range(groups):
            for s in range(blocks):
                source = places[slabs + s]
                row = (g * blocks + s) * GROUP
                scale = weights[g][source]
                for n in range(slabs):
                    share = shares[g][source * slabs + n].astype(F32)
                    for w in range(freqs):
                        weighted[w, row : row + GROUP, n * step : (n + 1) * step] = (
                            scale[:, w : w + 1] * share
                        ).astype(BF16)

    left = jnp.concatenate([t[...] for t in turned], axis=1)
    for w in range(freqs):
        out[w] = jnp.dot(left, weighted[w], preferred_element_type=F32).astype(BF16)


def respond(blocks, slabs, places, shares, weights, turned, vectors):
    groups = len(shares)
    columns, pairs = turned[0].shape
    freqs = weights[0].shape[2]
    height = min(columns, 256)
    smem = pl.BlockSpec(memory_space=pltpu.SMEM)
    vmem = pl.BlockSpec(memory_space=pltpu.VMEM)
    return pl.pallas_call(
        functools.partial(respond_kernel, blocks, slabs, groups, freqs),
        grid=(columns // height,),
        out_shape=jax.ShapeDtypeStruct((freqs, columns, vectors), BF16),
        in_specs=[smem]
        + [vmem] * (2 * groups)
        + [pl.BlockSpec((height, pairs), lambda i: (i, 0))] * groups,
        out_specs=pl.BlockSpec((freqs, height, vectors), lambda i: (0, i, 0)),
        scratch_shapes=[pltpu.VMEM((freqs, groups * pairs, vectors), BF16)],
        compiler_params=pltpu.CompilerParams(vmem_limit_bytes=VMEM),
        cost_estimate=pl.CostEstimate(
            flops=2 * groups * pairs * columns * vectors * freqs,
            bytes_accessed=2 * freqs * columns * vectors,
            transcendentals=0,
        ),
        name="respond",
    )(places, *shares, *weights, *turned)


def exchange(blocks, axis):
    size = len(blocks)
    if size > PERMUTE_MOST:
        return list(lax.all_to_all(jnp.stack(blocks), axis, 0, 0, tiled=True))
    return [blocks[0]] + [
        lax.ppermute(blocks[s], axis, [(i, i ^ s) for i in range(size)]) for s in range(1, size)
    ]


def partners(axis):
    size = lax.axis_size(axis)
    steps = jnp.arange(size, dtype=jnp.int32)
    return steps if size > PERMUTE_MOST else lax.axis_index(axis) ^ steps


def sum_shares(shares):
    both = ("wide", "narrow")
    count = shares.shape[0]
    taken = lax.all_to_all(shares, both, 0, 0, tiled=True)
    total = jnp.sum(taken.astype(F32), axis=0, keepdims=True)
    spread = jnp.broadcast_to(total, (count,) + total.shape[1:])
    return lax.all_to_all(spread, both, 0, 0, tiled=True)


def shards(occupied, empty, pair_occ, pair_emp, pair_level, denominators, trial):
    slabs = lax.axis_size("narrow")
    blocks = lax.axis_size("wide")
    grid = occupied.shape[1] * slabs
    zmat, ymat, xmat, swap = (jnp.asarray(t) for t in tables(grid, slabs))
    places = jnp.concatenate([partners("narrow"), partners("wide")])
    lanes = ymat.shape[1]
    groups = pair_occ.shape[0] // GROUP
    vectors = trial.shape[1]
    levels = jnp.arange(denominators.shape[0], dtype=jnp.int32)
    onehot = (pair_level[:, None] == levels[None, :]).astype(F32)
    weights = jnp.dot(onehot, denominators, precision=lax.Precision.HIGHEST)
    weights = weights.reshape(blocks, groups, GROUP, -1)

    shares, turned = [], []
    for g in range(groups):
        cut = SPLITS[g % len(SPLITS)]
        widths = tuple(lanes * c // sum(cut) for c in cut)
        sent = front(
            g * GROUP, slabs, widths, pair_occ, pair_emp, places, occupied, empty, zmat, ymat
        )
        parts, first = [], 0
        for h, wide in enumerate(widths):
            got = exchange(sent[h], "narrow")
            waves = across(slabs, blocks, first, grid, places, got, xmat, swap)
            parts += exchange(waves, "wide")
            first += wide
        share, turn = project(blocks, slabs, widths, places, trial, parts)
        shares.append(sum_shares(share))
        turned.append(turn)
    return respond(
        blocks,
        slabs,
        places,
        shares,
        [weights[:, g] for g in range(groups)],
        turned,
        vectors,
    )


def solution(mesh):
    placed = (
        P("wide", "narrow", None),
        P("wide", "narrow", None),
        P("wide"),
        P("wide"),
        P(),
        P(),
        P(("wide", "narrow"), None),
    )
    return jax.shard_map(
        shards,
        mesh=mesh,
        in_specs=placed,
        out_specs=P(None, ("wide", "narrow"), None),
        check_vma=False,
    )
```

```python
import functools
import math

import jax
import jax.numpy as jnp
import numpy as np
from jax import lax
from jax.experimental import pallas as pl
from jax.experimental.pallas import tpu as pltpu
from jax.sharding import PartitionSpec as P

GROUP = 16
LANES = 128
SPLITS = ((1,), (1,))
WHOLE = ((False,), (False,))
PERMUTE_MOST = 8
MIB = 1024 * 1024
COST = pl.CostEstimate(flops=1, bytes_accessed=1, transcendentals=0)
F32 = jnp.float32
BF16 = jnp.bfloat16


def rounded(values):
    return np.asarray(values, np.float32).astype(jnp.bfloat16)


def tables(grid, slabs):
    scaling = np.float32(1.0 / math.sqrt(grid))
    step = np.float32(2.0 * math.pi / grid)
    at = np.arange(grid)
    half = np.arange(grid // 2)

    def cos_sin(a, b):
        angle = (a[:, None] * b[None, :] % grid).astype(np.float32) * step
        return (
            rounded(np.cos(angle) * scaling).astype(np.float32),
            rounded(np.sin(angle) * scaling).astype(np.float32),
        )

    planes = grid // slabs
    depth = grid // 2 // slabs
    channels = 2 * depth
    group = LANES // channels
    zc, zs = cos_sin(at, half)
    ztab = np.stack([zc, -zs], -1).reshape(grid, slabs, channels)
    zmat = np.einsum("ab,znq->aznbq", np.eye(group, dtype=np.float32), ztab)
    zmat = zmat.reshape(group * grid, slabs * group * channels)
    signed = np.where(half < grid // 4, half, half - grid // 2)
    yc, ys = cos_sin(signed, at)
    mix = np.zeros((grid, 2, grid // 2, 2), np.float32)
    mix[:, 0, :, 0] = yc.T
    mix[:, 1, :, 0] = ys.T
    mix[:, 0, :, 1] = -ys.T
    mix[:, 1, :, 1] = yc.T
    ymat = np.einsum("yajb,dk->ydajkb", mix, np.eye(depth, dtype=np.float32))
    ymat = ymat.reshape(grid * channels, grid // 2 * channels)
    xc, xs = cos_sin(at, at)
    xtab = np.stack([xc, xs]).reshape(2, grid, slabs, planes)
    xmat = np.einsum("hksx,pr->skphrx", xtab, np.eye(8, dtype=np.float32))
    xmat = xmat.reshape(slabs, grid * 8, 2 * 8 * planes)
    swap = np.zeros((2 * LANES, 2 * LANES), np.float32)
    even = np.arange(0, 2 * LANES, 2)
    swap[even + 1, even] = 1.0
    swap[even, even + 1] = -1.0
    return rounded(zmat), rounded(ymat), rounded(xmat), rounded(swap)


def partners(slabs, blocks):
    narrow, wide = lax.axis_index("narrow"), lax.axis_index("wide")
    return [narrow ^ s for s in range(slabs)] + [wide ^ s for s in range(blocks)]


def views(refs, places, first, count):
    found = []
    for ref in refs:
        if len(ref.shape) == 3:
            found += [ref.at[places[first + s]] for s in range(count)]
        else:
            found.append(ref)
    return found


def shapes(count, height, wide, whole):
    if whole or count > PERMUTE_MOST:
        return [jax.ShapeDtypeStruct((count, height, wide), BF16)]
    return [jax.ShapeDtypeStruct((height, wide), BF16)] * count


def front_kernel(start, slabs, widths, occ_at, emp_at, *rest):
    count = len(rest) - 11
    outs, (prod, lines) = rest[4 : 4 + count], rest[4 + count : 6 + count]
    held, arrived = rest[6 + count : 10 + count], rest[10 + count]
    occ, emp, zmat, ymat = held
    planes = occ.shape[1]
    width = zmat.shape[0]
    steps = occ.shape[2] // width
    mats = [pltpu.make_async_copy(rest[2 + i], held[2 + i], arrived.at[i]) for i in range(2)]
    pieces = []
    for g in range(steps):
        lanes = slice(g * width, (g + 1) * width)
        pieces.append(
            [
                pltpu.make_async_copy(
                    rest[i].at[:, :, lanes], held[i].at[:, :, lanes], arrived.at[2 + 2 * g + i]
                )
                for i in range(2)
            ]
        )
    pieces[0][0].start()
    pieces[0][1].start()
    mats[0].start()
    for piece in pieces[1:]:
        piece[0].start()
        piece[1].start()
    mats[1].start()
    places = partners(slabs, 1)
    outs = views(outs, places, 0, slabs)
    for g in range(steps):
        lanes = slice(g * width, (g + 1) * width)
        pieces[g][0].wait()
        pieces[g][1].wait()
        for p in range(GROUP):
            o, e = occ_at[start + p], emp_at[start + p]
            prod[p * planes : (p + 1) * planes, :] = (
                occ[o, :, lanes].astype(F32) * emp[e, :, lanes].astype(F32)
            ).astype(BF16)
        if g == 0:
            mats[0].wait()
        along = jnp.dot(prod[...], zmat[...], preferred_element_type=F32).astype(BF16)
        for n in range(slabs):
            lines[n, :, g * LANES : (g + 1) * LANES] = along[:, n * LANES : (n + 1) * LANES]
    mats[1].wait()
    for s in range(slabs):
        along = jnp.dot(lines[places[s]], ymat[...], preferred_element_type=F32).astype(BF16)
        first = 0
        for h, wide in enumerate(widths):
            outs[h * slabs + s][...] = along[:, first : first + wide]
            first += wide


def front(start, slabs, widths, occ_at, emp_at, *held):
    occ, _, zmat, ymat = held
    rows = GROUP * occ.shape[1]
    width = zmat.shape[0]
    steps = occ.shape[2] // width
    smem = pl.BlockSpec(memory_space=pltpu.SMEM)
    vmem = pl.BlockSpec(memory_space=pltpu.VMEM)
    out_shape = [o for w in widths for o in shapes(slabs, rows, w, False)]
    outs = pl.pallas_call(
        functools.partial(front_kernel, start, slabs, widths),
        out_shape=out_shape,
        in_specs=[smem] * 2 + [pl.BlockSpec(memory_space=pl.ANY)] * 4,
        out_specs=[vmem] * len(out_shape),
        scratch_shapes=[
            pltpu.VMEM((rows, width), BF16),
            pltpu.VMEM((slabs, rows, ymat.shape[0]), BF16),
        ]
        + [pltpu.VMEM(h.shape, BF16) for h in held]
        + [pltpu.SemaphoreType.DMA((2 + 2 * steps,))],
        compiler_params=pltpu.CompilerParams(vmem_limit_bytes=56 * MIB),
        cost_estimate=COST,
        name="front",
    )(occ_at, emp_at, *held)
    each = len(outs) // len(widths)
    return [outs[h * each : (h + 1) * each] for h in range(len(widths))]


def across_kernel(slabs, blocks, first, grid, taken, after, *rest):
    places = partners(slabs, blocks)
    parts = views(rest[:taken], places, 0, slabs)
    xmat, swap = rest[taken : taken + 2]
    outs, whole = views(rest[taken + 2 + after : -1], places, slabs, blocks), rest[-1]
    rows, wide = parts[0].shape
    planes = rows // GROUP
    half = grid // 2
    channels = 2 * (half // slabs)
    lane = first + lax.broadcasted_iota(jnp.int32, (grid, wide), 1)
    kx = lax.broadcasted_iota(jnp.int32, (grid, wide), 0)
    kx = jnp.where(kx < half, kx, kx - grid)
    ky = lane // channels
    ky = jnp.where(ky < half // 2, ky, ky - half)
    kz = places[0] * (channels // 2) + lane % channels // 2
    squared = (kx * kx + ky * ky + kz * kz).astype(F32)
    quarter = float(grid // 4)
    coulomb = (1.0 / jnp.sqrt(1.0 + squared / (quarter * quarter)))[:, None, :]
    left = jnp.concatenate([xmat[places[s]] for s in range(slabs)], axis=1)
    found = []
    for m in range(GROUP // 8):
        right = []
        for s in range(slabs):
            plain = parts[s][m * 8 * planes : (m + 1) * 8 * planes, :]
            right.append(plain)
            turned = [
                jnp.dot(plain[:, c : c + 2 * LANES], swap[...], preferred_element_type=F32)
                for c in range(0, wide, 2 * LANES)
            ]
            right.append(jnp.concatenate(turned, axis=1).astype(BF16))
        right = jnp.concatenate(right, axis=0)
        total = jnp.dot(left, right, preferred_element_type=F32)
        found.append(total.reshape(grid, 8, wide) * coulomb)
    found = jnp.concatenate(found, axis=1).astype(BF16)
    whole[...] = found.reshape(whole.shape)
    for s in range(blocks):
        outs[s][...] = whole[places[slabs + s]]


def across(slabs, blocks, first, grid, parts, xmat, swap, whole, after):
    rows, wide = parts[0].shape[-2:]
    tall = grid // blocks * GROUP
    out_shape = shapes(blocks, tall, wide, whole)
    vmem = pl.BlockSpec(memory_space=pltpu.VMEM)
    return pl.pallas_call(
        functools.partial(across_kernel, slabs, blocks, first, grid, len(parts), len(after)),
        out_shape=out_shape,
        in_specs=[vmem] * (len(parts) + 2)
        + [pl.BlockSpec(memory_space=pl.ANY)] * len(after),
        out_specs=[vmem] * len(out_shape),
        scratch_shapes=[pltpu.VMEM((blocks, tall, wide), BF16)],
        compiler_params=pltpu.CompilerParams(vmem_limit_bytes=24 * MIB),
        cost_estimate=COST,
        name="across",
    )(*parts, xmat, swap, *after)


def project_kernel(blocks, slabs, widths, after, held, trial, *rest):
    shares = rest[-1]
    parts, earlier = rest[: -1 - after - held], rest[-1 - after - held : -1 - after]
    places = partners(slabs, blocks)
    parts = views(parts, places, slabs, blocks)
    for ref in earlier:
        shares[:, : ref.shape[1], :] = ref[...]
    below = shares.shape[1] - GROUP
    lanes = sum(widths)
    heights = parts[0].shape[0] // GROUP
    total = jnp.zeros((blocks * GROUP, trial.shape[1]), F32)
    for x in range(heights):
        first = x * lanes
        for h, wide in enumerate(widths):
            left = jnp.concatenate(
                [parts[h * blocks + s][x * GROUP : (x + 1) * GROUP, :] for s in range(blocks)], axis=0
            )
            total += jnp.dot(left, trial[first : first + wide, :], preferred_element_type=F32)
            first += wide
    step = trial.shape[1] // slabs
    for s in range(blocks):
        for n in range(slabs):
            shares[places[slabs + s] * slabs + n, below:, :] = total[
                s * GROUP : (s + 1) * GROUP, n * step : (n + 1) * step
            ].astype(shares.dtype)


def project(blocks, slabs, widths, trial, parts, earlier, after):
    columns, vectors = trial.shape
    pairs = blocks * GROUP
    height = GROUP + sum(e.shape[1] for e in earlier)
    vmem = pl.BlockSpec(memory_space=pltpu.VMEM)
    return pl.pallas_call(
        functools.partial(project_kernel, blocks, slabs, widths, len(after), len(earlier)),
        out_shape=jax.ShapeDtypeStruct((blocks * slabs, height, vectors // slabs), BF16),
        in_specs=[vmem] * (1 + len(parts) + len(earlier))
        + [pl.BlockSpec(memory_space=pl.ANY)] * len(after),
        out_specs=vmem,
        compiler_params=pltpu.CompilerParams(vmem_limit_bytes=24 * MIB),
        cost_estimate=COST,
        name="project",
    )(trial, *parts, *earlier, *after)


def turn_kernel(blocks, slabs, widths, *rest):
    places = partners(slabs, blocks)
    parts, turned = views(rest[:-1], places, slabs, blocks), rest[-1]
    lanes = sum(widths)
    for x in range(parts[0].shape[0] // GROUP):
        first = x * lanes
        for h, wide in enumerate(widths):
            left = [parts[h * blocks + s][x * GROUP : (x + 1) * GROUP, :] for s in range(blocks)]
            turned[first : first + wide, :] = jnp.concatenate(left, axis=0).T
            first += wide


def turn(blocks, slabs, widths, columns, parts):
    vmem = pl.BlockSpec(memory_space=pltpu.VMEM)
    return pl.pallas_call(
        functools.partial(turn_kernel, blocks, slabs, widths),
        out_shape=jax.ShapeDtypeStruct((columns, blocks * GROUP), BF16),
        in_specs=[vmem] * len(parts),
        out_specs=vmem,
        compiler_params=pltpu.CompilerParams(vmem_limit_bytes=16 * MIB),
        cost_estimate=COST,
        name="turn",
    )(*parts)


def respond_kernel(blocks, slabs, groups, freqs, *rest):
    shares, weights, turned = rest[0], rest[1], rest[2 : groups + 2]
    out, weighted = rest[groups + 2 :]
    places = partners(slabs, blocks)
    vectors = out.shape[2]
    step = vectors // slabs

    @pl.when(pl.program_id(0) == 0)
    def _():
        for g in range(groups):
            for s in range(blocks):
                source = places[slabs + s]
                row = (g * blocks + s) * GROUP
                scale = weights[source, g]
                for n in range(slabs):
                    share = shares[source * slabs + n, g * GROUP : (g + 1) * GROUP, :].astype(F32)
                    for w in range(freqs):
                        weighted[w, row : row + GROUP, n * step : (n + 1) * step] = (
                            scale[:, w : w + 1] * share
                        ).astype(BF16)

    left = jnp.concatenate([t[...] for t in turned], axis=1)
    for w in range(freqs):
        out[w] = jnp.dot(left, weighted[w], preferred_element_type=F32).astype(BF16)


def respond(blocks, slabs, shares, weights, turned, vectors):
    groups = len(turned)
    columns, pairs = turned[0].shape
    freqs = weights.shape[-1]
    height = min(columns, 512)
    vmem = pl.BlockSpec(memory_space=pltpu.VMEM)
    return pl.pallas_call(
        functools.partial(respond_kernel, blocks, slabs, groups, freqs),
        grid=(columns // height,),
        out_shape=jax.ShapeDtypeStruct((freqs, columns, vectors), BF16),
        in_specs=[vmem] * 2
        + [pl.BlockSpec((height, pairs), lambda i: (i, 0))] * groups,
        out_specs=pl.BlockSpec((freqs, height, vectors), lambda i: (0, i, 0)),
        scratch_shapes=[pltpu.VMEM((freqs, groups * pairs, vectors), BF16)],
        compiler_params=pltpu.CompilerParams(vmem_limit_bytes=16 * MIB + 4 * freqs * vectors * (groups * pairs + height)),
        cost_estimate=COST,
        name="respond",
    )(shares, weights, *turned)


def exchange(blocks, axis):
    if len(blocks) == 1:
        return [lax.all_to_all(blocks[0], axis, 0, 0, tiled=True)]
    return [blocks[0]] + [
        lax.ppermute(blocks[s], axis, [(i, i ^ s) for i in range(len(blocks))])
        for s in range(1, len(blocks))
    ]


def sum_shares(shares):
    both = ("wide", "narrow")
    count = shares.shape[0]
    taken = lax.all_to_all(shares, both, 0, 0, tiled=True)
    total = jnp.sum(taken.astype(F32), axis=0, keepdims=True).astype(BF16)
    spread = jnp.broadcast_to(total, (count,) + total.shape[1:])
    return lax.all_to_all(spread, both, 0, 0, tiled=True)


def shards(occupied, empty, pair_occ, pair_emp, pair_level, denominators, trial):
    slabs = lax.axis_size("narrow")
    blocks = lax.axis_size("wide")
    grid = occupied.shape[1] * slabs
    zmat, ymat, xmat, swap = (jnp.asarray(t) for t in tables(grid, slabs))
    lanes = ymat.shape[1]
    groups = pair_occ.shape[0] // GROUP
    vectors = trial.shape[1]
    levels = jnp.arange(denominators.shape[0], dtype=jnp.int32)
    onehot = (pair_level[:, None] == levels[None, :]).astype(F32)
    weights = jnp.dot(onehot, denominators, precision=lax.Precision.HIGHEST)
    weights = weights.reshape(blocks, groups, GROUP, -1)

    sent, waves = {}, {}
    for g in range(groups):
        cut = SPLITS[g % len(SPLITS)]
        widths = tuple(lanes * c // sum(cut) for c in cut)
        sent[g] = widths, front(
            g * GROUP, slabs, widths, pair_occ, pair_emp, occupied, empty, zmat, ymat
        )
    for g in range(groups):
        first, waves[g] = 0, []
        after = [blocked[0] for blocked in sent[g + 1][1]] if g + 1 < groups else []
        for whole, wide, blocked in zip(WHOLE[g % len(WHOLE)], *sent[g]):
            got = exchange(blocked, "narrow")
            waves[g].append(
                across(slabs, blocks, first, grid, got, xmat, swap, whole, after)
            )
            first += wide
    shares, turned = [], []
    for g in range(groups):
        parts = [piece for blocked in waves[g] for piece in exchange(blocked, "wide")]
        after = [blocked[0] for blocked in waves.get(g + 1, [])]
        widths = sent[g][0]
        shares = [project(blocks, slabs, widths, trial, parts, shares, after)]
        turned.append(turn(blocks, slabs, widths, trial.shape[0], parts))
    shares = sum_shares(shares[0])
    return respond(
        blocks,
        slabs,
        shares,
        weights,
        turned,
        vectors,
    )


def solution(mesh):
    placed = (
        P("wide", "narrow", None),
        P("wide", "narrow", None),
        P("wide"),
        P("wide"),
        P(),
        P(),
        P(("wide", "narrow"), None),
    )
    return jax.shard_map(
        shards,
        mesh=mesh,
        in_specs=placed,
        out_specs=P(None, ("wide", "narrow"), None),
        check_vma=False,
    )
```

```python
import functools
import math

import jax
import jax.numpy as jnp
import numpy as np
from jax import lax
from jax.experimental import pallas as pl
from jax.experimental.pallas import tpu as pltpu
from jax.sharding import PartitionSpec as P

GROUP = 16
LANES = 128
SPLITS = ((1,), (1,))
PERMUTE_MOST = 8
MIB = 1024 * 1024
COST = pl.CostEstimate(flops=1, bytes_accessed=1, transcendentals=0)
F32 = jnp.float32
BF16 = jnp.bfloat16


def rounded(values):
    return np.asarray(values, np.float32).astype(jnp.bfloat16)


def tables(grid, slabs):
    scaling = np.float32(1.0 / math.sqrt(grid))
    step = np.float32(2.0 * math.pi / grid)
    at = np.arange(grid)
    half = np.arange(grid // 2)

    def cos_sin(a, b):
        angle = (a[:, None] * b[None, :] % grid).astype(np.float32) * step
        return (
            rounded(np.cos(angle) * scaling).astype(np.float32),
            rounded(np.sin(angle) * scaling).astype(np.float32),
        )

    planes = grid // slabs
    depth = grid // 2 // slabs
    channels = 2 * depth
    group = LANES // channels
    zc, zs = cos_sin(at, half)
    ztab = np.stack([zc, -zs], -1).reshape(grid, slabs, channels)
    zmat = np.einsum("ab,znq->aznbq", np.eye(group, dtype=np.float32), ztab)
    zmat = zmat.reshape(group * grid, slabs * group * channels)
    signed = np.where(half < grid // 4, half, half - grid // 2)
    yc, ys = cos_sin(signed, at)
    mix = np.zeros((grid, 2, grid // 2, 2), np.float32)
    mix[:, 0, :, 0] = yc.T
    mix[:, 1, :, 0] = ys.T
    mix[:, 0, :, 1] = -ys.T
    mix[:, 1, :, 1] = yc.T
    ymat = np.einsum("yajb,dk->ydajkb", mix, np.eye(depth, dtype=np.float32))
    ymat = ymat.reshape(grid * channels, grid // 2 * channels)
    xc, xs = cos_sin(at, at)
    xtab = np.stack([xc, xs]).reshape(2, grid, slabs, planes)
    xmat = np.einsum("hksx,pr->skphrx", xtab, np.eye(8, dtype=np.float32))
    xmat = xmat.reshape(slabs, grid * 8, 2 * 8 * planes)
    swap = np.zeros((2 * LANES, 2 * LANES), np.float32)
    even = np.arange(0, 2 * LANES, 2)
    swap[even + 1, even] = 1.0
    swap[even, even + 1] = -1.0
    return rounded(zmat), rounded(ymat), rounded(xmat), rounded(swap)


def partners(slabs, blocks):
    narrow, wide = lax.axis_index("narrow"), lax.axis_index("wide")
    return [narrow ^ s for s in range(slabs)] + [wide ^ s for s in range(blocks)]


def views(refs, places, first, count):
    found = []
    for ref in refs:
        if len(ref.shape) == 3:
            found += [ref.at[places[first + s]] for s in range(count)]
        else:
            found.append(ref)
    return found


def shapes(count, height, wide, whole):
    if whole or count > PERMUTE_MOST:
        return [jax.ShapeDtypeStruct((count, height, wide), BF16)]
    return [jax.ShapeDtypeStruct((height, wide), BF16)] * count


def front_kernel(start, slabs, widths, occ_at, emp_at, *rest):
    count = len(rest) - 11
    outs, (prod, lines) = rest[4 : 4 + count], rest[4 + count : 6 + count]
    held, arrived = rest[6 + count : 10 + count], rest[10 + count]
    occ, emp, zmat, ymat = held
    planes = occ.shape[1]
    width = zmat.shape[0]
    steps = occ.shape[2] // width
    mats = [pltpu.make_async_copy(rest[2 + i], held[2 + i], arrived.at[i]) for i in range(2)]
    pieces = []
    for g in range(steps):
        lanes = slice(g * width, (g + 1) * width)
        pieces.append(
            [
                pltpu.make_async_copy(
                    rest[i].at[:, :, lanes], held[i].at[:, :, lanes], arrived.at[2 + 2 * g + i]
                )
                for i in range(2)
            ]
        )
    pieces[0][0].start()
    pieces[0][1].start()
    mats[0].start()
    for piece in pieces[1:]:
        piece[0].start()
        piece[1].start()
    mats[1].start()
    places = partners(slabs, 1)
    outs = views(outs, places, 0, slabs)
    chosen = [(occ_at[start + p], emp_at[start + p]) for p in range(GROUP)]
    for g in range(steps):
        lanes = slice(g * width, (g + 1) * width)
        pieces[g][0].wait()
        pieces[g][1].wait()
        for p in range(GROUP):
            o, e = chosen[p]
            prod[p * planes : (p + 1) * planes, :] = (
                occ[o, :, lanes].astype(F32) * emp[e, :, lanes].astype(F32)
            ).astype(BF16)
        if g == 0:
            mats[0].wait()
        along = jnp.dot(prod[...], zmat[...], preferred_element_type=F32).astype(BF16)
        for n in range(slabs):
            lines[n, :, g * LANES : (g + 1) * LANES] = along[:, n * LANES : (n + 1) * LANES]
    mats[1].wait()
    for s in range(slabs):
        along = jnp.dot(lines[places[s]], ymat[...], preferred_element_type=F32).astype(BF16)
        first = 0
        for h, wide in enumerate(widths):
            outs[h * slabs + s][...] = along[:, first : first + wide]
            first += wide


def front(start, slabs, widths, occ_at, emp_at, *held):
    occ, _, zmat, ymat = held
    rows = GROUP * occ.shape[1]
    width = zmat.shape[0]
    steps = occ.shape[2] // width
    smem = pl.BlockSpec(memory_space=pltpu.SMEM)
    vmem = pl.BlockSpec(memory_space=pltpu.VMEM)
    out_shape = [o for w in widths for o in shapes(slabs, rows, w, False)]
    outs = pl.pallas_call(
        functools.partial(front_kernel, start, slabs, widths),
        out_shape=out_shape,
        in_specs=[smem] * 2 + [pl.BlockSpec(memory_space=pl.ANY)] * 4,
        out_specs=[vmem] * len(out_shape),
        scratch_shapes=[
            pltpu.VMEM((rows, width), BF16),
            pltpu.VMEM((slabs, rows, ymat.shape[0]), BF16),
        ]
        + [pltpu.VMEM(h.shape, BF16) for h in held]
        + [pltpu.SemaphoreType.DMA((2 + 2 * steps,))],
        compiler_params=pltpu.CompilerParams(vmem_limit_bytes=56 * MIB),
        cost_estimate=COST,
        name="front",
    )(occ_at, emp_at, *held)
    each = len(outs) // len(widths)
    return [outs[h * each : (h + 1) * each] for h in range(len(widths))]


def across_kernel(slabs, blocks, first, grid, part, taken, after, *rest):
    places = partners(slabs, blocks)
    parts = views(rest[:taken], places, 0, slabs)
    xmat, swap = rest[taken : taken + 2]
    outs, whole = views(rest[taken + 2 + after : -1], places, slabs, blocks), rest[-1]
    count = whole.shape[0]
    half = 0 if part is None else places[slabs] // count ^ part
    tall = grid // blocks * count
    rows, wide = parts[0].shape
    planes = rows // GROUP
    channels = grid // slabs
    lane = first + lax.broadcasted_iota(jnp.int32, (tall, wide), 1)
    kx = half * tall + lax.broadcasted_iota(jnp.int32, (tall, wide), 0)
    kx = jnp.where(kx < grid // 2, kx, kx - grid)
    ky = lane // channels
    ky = jnp.where(ky < grid // 4, ky, ky - grid // 2)
    kz = places[0] * (channels // 2) + lane % channels // 2
    squared = (kx * kx + ky * ky + kz * kz).astype(F32)
    quarter = float(grid // 4)
    coulomb = (1.0 / jnp.sqrt(1.0 + squared / (quarter * quarter)))[:, None, :]
    rows_here = pl.ds(half * (8 * tall), 8 * tall)
    left = jnp.concatenate([xmat[places[s], rows_here, :] for s in range(slabs)], axis=1)
    found = []
    for m in range(GROUP // 8):
        right = []
        for s in range(slabs):
            plain = parts[s][m * 8 * planes : (m + 1) * 8 * planes, :]
            right.append(plain)
            turned = [
                jnp.dot(plain[:, c : c + 2 * LANES], swap[...], preferred_element_type=F32)
                for c in range(0, wide, 2 * LANES)
            ]
            right.append(jnp.concatenate(turned, axis=1).astype(BF16))
        right = jnp.concatenate(right, axis=0)
        total = jnp.dot(left, right, preferred_element_type=F32)
        found.append(total.reshape(tall, 8, wide) * coulomb)
    found = jnp.concatenate(found, axis=1).astype(BF16)
    whole[...] = found.reshape(whole.shape)
    for i in range(count):
        at = places[slabs + (part or 0) * count + i]
        outs[i][...] = whole[at - half * count]


def across(slabs, blocks, first, grid, parts, xmat, swap, part, after):
    rows, wide = parts[0].shape[-2:]
    tall = grid // blocks * GROUP
    count = blocks if part is None else blocks // 2
    out_shape = shapes(count, tall, wide, part is None)
    vmem = pl.BlockSpec(memory_space=pltpu.VMEM)
    return pl.pallas_call(
        functools.partial(across_kernel, slabs, blocks, first, grid, part, len(parts), len(after)),
        out_shape=out_shape,
        in_specs=[vmem] * (len(parts) + 2)
        + [pl.BlockSpec(memory_space=pl.ANY)] * len(after),
        out_specs=[vmem] * len(out_shape),
        scratch_shapes=[pltpu.VMEM((count, tall, wide), BF16)],
        compiler_params=pltpu.CompilerParams(vmem_limit_bytes=24 * MIB),
        cost_estimate=COST,
        name="across",
    )(*parts, xmat, swap, *after)


def project_kernel(blocks, slabs, widths, after, held, trial, *rest):
    shares = rest[-1]
    parts, earlier = rest[: -1 - after - held], rest[-1 - after - held : -1 - after]
    places = partners(slabs, blocks)
    parts = views(parts, places, slabs, blocks)
    for ref in earlier:
        shares[:, : ref.shape[1], :] = ref[...]
    below = shares.shape[1] - GROUP
    lanes = sum(widths)
    heights = parts[0].shape[0] // GROUP
    total = jnp.zeros((blocks * GROUP, trial.shape[1]), F32)
    for x in range(heights):
        first = x * lanes
        for h, wide in enumerate(widths):
            left = jnp.concatenate(
                [parts[h * blocks + s][x * GROUP : (x + 1) * GROUP, :] for s in range(blocks)], axis=0
            )
            total += jnp.dot(left, trial[first : first + wide, :], preferred_element_type=F32)
            first += wide
    step = trial.shape[1] // slabs
    for s in range(blocks):
        for n in range(slabs):
            shares[places[slabs + s] * slabs + n, below:, :] = total[
                s * GROUP : (s + 1) * GROUP, n * step : (n + 1) * step
            ].astype(shares.dtype)


def project(blocks, slabs, widths, trial, parts, earlier, after):
    columns, vectors = trial.shape
    pairs = blocks * GROUP
    height = GROUP + sum(e.shape[1] for e in earlier)
    vmem = pl.BlockSpec(memory_space=pltpu.VMEM)
    return pl.pallas_call(
        functools.partial(project_kernel, blocks, slabs, widths, len(after), len(earlier)),
        out_shape=jax.ShapeDtypeStruct((blocks * slabs, height, vectors // slabs), BF16),
        in_specs=[vmem] * (1 + len(parts) + len(earlier))
        + [pl.BlockSpec(memory_space=pl.ANY)] * len(after),
        out_specs=vmem,
        compiler_params=pltpu.CompilerParams(vmem_limit_bytes=24 * MIB),
        cost_estimate=COST,
        name="project",
    )(trial, *parts, *earlier, *after)


def turn_kernel(blocks, slabs, widths, *rest):
    places = partners(slabs, blocks)
    parts, turned = views(rest[:-1], places, slabs, blocks), rest[-1]
    lanes = sum(widths)
    for x in range(parts[0].shape[0] // GROUP):
        first = x * lanes
        for h, wide in enumerate(widths):
            left = [parts[h * blocks + s][x * GROUP : (x + 1) * GROUP, :] for s in range(blocks)]
            turned[first : first + wide, :] = jnp.concatenate(left, axis=0).T
            first += wide


def turn(blocks, slabs, widths, columns, parts):
    vmem = pl.BlockSpec(memory_space=pltpu.VMEM)
    return pl.pallas_call(
        functools.partial(turn_kernel, blocks, slabs, widths),
        out_shape=jax.ShapeDtypeStruct((columns, blocks * GROUP), BF16),
        in_specs=[vmem] * len(parts),
        out_specs=vmem,
        compiler_params=pltpu.CompilerParams(vmem_limit_bytes=16 * MIB),
        cost_estimate=COST,
        name="turn",
    )(*parts)


def respond_kernel(blocks, slabs, groups, freqs, *rest):
    shares, weights, turned = rest[0], rest[1], rest[2 : groups + 2]
    out, weighted = rest[groups + 2 :]
    places = partners(slabs, blocks)
    vectors = out.shape[2]
    step = vectors // slabs

    @pl.when(pl.program_id(0) == 0)
    def _():
        for g in range(groups):
            for s in range(blocks):
                source = places[slabs + s]
                row = (g * blocks + s) * GROUP
                scale = weights[source, g]
                for n in range(slabs):
                    share = shares[source * slabs + n, g * GROUP : (g + 1) * GROUP, :].astype(F32)
                    for w in range(freqs):
                        weighted[w, row : row + GROUP, n * step : (n + 1) * step] = (
                            scale[:, w : w + 1] * share
                        ).astype(BF16)

    left = jnp.concatenate([t[...] for t in turned], axis=1)
    for w in range(freqs):
        out[w] = jnp.dot(left, weighted[w], preferred_element_type=F32).astype(BF16)


def respond(blocks, slabs, shares, weights, turned, vectors):
    groups = len(turned)
    columns, pairs = turned[0].shape
    freqs = weights.shape[-1]
    height = min(columns, 512)
    vmem = pl.BlockSpec(memory_space=pltpu.VMEM)
    return pl.pallas_call(
        functools.partial(respond_kernel, blocks, slabs, groups, freqs),
        grid=(columns // height,),
        out_shape=jax.ShapeDtypeStruct((freqs, columns, vectors), BF16),
        in_specs=[vmem] * 2
        + [pl.BlockSpec((height, pairs), lambda i: (i, 0))] * groups,
        out_specs=pl.BlockSpec((freqs, height, vectors), lambda i: (0, i, 0)),
        scratch_shapes=[pltpu.VMEM((freqs, groups * pairs, vectors), BF16)],
        compiler_params=pltpu.CompilerParams(vmem_limit_bytes=16 * MIB + 4 * freqs * vectors * (groups * pairs + height)),
        cost_estimate=COST,
        name="respond",
    )(shares, weights, *turned)


def exchange(blocks, axis):
    if len(blocks) == 1:
        return [lax.all_to_all(blocks[0], axis, 0, 0, tiled=True)]
    return [blocks[0]] + [
        lax.ppermute(blocks[s], axis, [(i, i ^ s) for i in range(len(blocks))])
        for s in range(1, len(blocks))
    ]


def sum_shares(shares):
    both = ("wide", "narrow")
    count = shares.shape[0]
    taken = lax.all_to_all(shares, both, 0, 0, tiled=True)
    total = jnp.sum(taken.astype(F32), axis=0, keepdims=True).astype(BF16)
    spread = jnp.broadcast_to(total, (count,) + total.shape[1:])
    return lax.all_to_all(spread, both, 0, 0, tiled=True)


def shards(occupied, empty, pair_occ, pair_emp, pair_level, denominators, trial):
    slabs = lax.axis_size("narrow")
    blocks = lax.axis_size("wide")
    grid = occupied.shape[1] * slabs
    zmat, ymat, xmat, swap = (jnp.asarray(t) for t in tables(grid, slabs))
    lanes = ymat.shape[1]
    groups = pair_occ.shape[0] // GROUP
    vectors = trial.shape[1]
    levels = jnp.arange(denominators.shape[0], dtype=jnp.int32)
    onehot = (pair_level[:, None] == levels[None, :]).astype(F32)
    weights = jnp.dot(onehot, denominators, precision=lax.Precision.HIGHEST)
    weights = weights.reshape(blocks, groups, GROUP, -1)

    sent, waves = {}, {}
    for g in range(groups):
        cut = SPLITS[g % len(SPLITS)]
        widths = tuple(lanes * c // sum(cut) for c in cut)
        sent[g] = widths, front(
            g * GROUP, slabs, widths, pair_occ, pair_emp, occupied, empty, zmat, ymat
        )
    for g in range(groups):
        first, waves[g] = 0, []
        after = [blocked[0] for blocked in sent[g + 1][1]] if g + 1 < groups else []
        for wide, blocked in zip(*sent[g]):
            got = exchange(blocked, "narrow")
            if blocks > PERMUTE_MOST:
                stack = across(slabs, blocks, first, grid, got, xmat, swap, None, after)
                waves[g].append(stack)
            else:
                far = across(slabs, blocks, first, grid, got, xmat, swap, 1, after)
                near = across(slabs, blocks, first, grid, got, xmat, swap, 0, far[:1])
                waves[g].append(list(near) + list(far))
            first += wide
    shares, turned = [], []
    for g in range(groups):
        parts = [piece for blocked in waves[g] for piece in exchange(blocked, "wide")]
        after = [blocked[0] for blocked in waves.get(g + 1, [])]
        widths = sent[g][0]
        shares = [project(blocks, slabs, widths, trial, parts, shares, after)]
        turned.append(turn(blocks, slabs, widths, trial.shape[0], parts))
    shares = sum_shares(shares[0])
    return respond(
        blocks,
        slabs,
        shares,
        weights,
        turned,
        vectors,
    )


def solution(mesh):
    placed = (
        P("wide", "narrow", None),
        P("wide", "narrow", None),
        P("wide"),
        P("wide"),
        P(),
        P(),
        P(("wide", "narrow"), None),
    )
    return jax.shard_map(
        shards,
        mesh=mesh,
        in_specs=placed,
        out_specs=P(None, ("wide", "narrow"), None),
        check_vma=False,
    )
```

```python
import functools
import math

import jax
import jax.numpy as jnp
import numpy as np
from jax import lax
from jax.experimental import pallas as pl
from jax.experimental.pallas import tpu as pltpu
from jax.sharding import PartitionSpec as P

GROUP = 16
LANES = 128
SPLITS = ((1,), (1,))
PERMUTE_MOST = 8
MIB = 1024 * 1024
COST = pl.CostEstimate(flops=1, bytes_accessed=1, transcendentals=0)
F32 = jnp.float32
BF16 = jnp.bfloat16


def rounded(values):
    return np.asarray(values, np.float32).astype(jnp.bfloat16)


def tables(grid, slabs):
    scaling = np.float32(1.0 / math.sqrt(grid))
    step = np.float32(2.0 * math.pi / grid)
    at = np.arange(grid)
    half = np.arange(grid // 2)

    def cos_sin(a, b):
        angle = (a[:, None] * b[None, :] % grid).astype(np.float32) * step
        return (
            rounded(np.cos(angle) * scaling).astype(np.float32),
            rounded(np.sin(angle) * scaling).astype(np.float32),
        )

    planes = grid // slabs
    depth = grid // 2 // slabs
    channels = 2 * depth
    group = LANES // channels
    zc, zs = cos_sin(at, half)
    ztab = np.stack([zc, -zs], -1).reshape(grid, slabs, channels)
    zmat = np.einsum("ab,znq->aznbq", np.eye(group, dtype=np.float32), ztab)
    zmat = zmat.reshape(group * grid, slabs * group * channels)
    signed = np.where(half < grid // 4, half, half - grid // 2)
    yc, ys = cos_sin(signed, at)
    mix = np.zeros((grid, 2, grid // 2, 2), np.float32)
    mix[:, 0, :, 0] = yc.T
    mix[:, 1, :, 0] = ys.T
    mix[:, 0, :, 1] = -ys.T
    mix[:, 1, :, 1] = yc.T
    ymat = np.einsum("yajb,dk->ydajkb", mix, np.eye(depth, dtype=np.float32))
    ymat = ymat.reshape(grid * channels, grid // 2 * channels)
    xc, xs = cos_sin(at, at)
    xtab = np.stack([xc, xs]).reshape(2, grid, slabs, planes)
    xmat = np.einsum("hksx,pr->skphrx", xtab, np.eye(8, dtype=np.float32))
    xmat = xmat.reshape(slabs, grid * 8, 2 * 8 * planes)
    swap = np.zeros((2 * LANES, 2 * LANES), np.float32)
    even = np.arange(0, 2 * LANES, 2)
    swap[even + 1, even] = 1.0
    swap[even, even + 1] = -1.0
    return rounded(zmat), rounded(ymat), rounded(xmat), rounded(swap)


def partners(slabs, blocks):
    narrow, wide = lax.axis_index("narrow"), lax.axis_index("wide")
    return [narrow ^ s for s in range(slabs)] + [wide ^ s for s in range(blocks)]


def views(refs, places, first, count):
    found = []
    for ref in refs:
        if len(ref.shape) == 3:
            found += [ref.at[places[first + s]] for s in range(count)]
        else:
            found.append(ref)
    return found


def shapes(count, height, wide, whole):
    if whole or count > PERMUTE_MOST:
        return [jax.ShapeDtypeStruct((count, height, wide), BF16)]
    return [jax.ShapeDtypeStruct((height, wide), BF16)] * count


def front_kernel(start, slabs, widths, occ_at, emp_at, *rest):
    count = len(rest) - 11
    outs, (prod, lines) = rest[4 : 4 + count], rest[4 + count : 6 + count]
    held, arrived = rest[6 + count : 10 + count], rest[10 + count]
    occ, emp, zmat, ymat = held
    planes = occ.shape[1]
    width = zmat.shape[0]
    steps = occ.shape[2] // width
    mats = [pltpu.make_async_copy(rest[2 + i], held[2 + i], arrived.at[i]) for i in range(2)]
    pieces = []
    for g in range(steps):
        lanes = slice(g * width, (g + 1) * width)
        pieces.append(
            [
                pltpu.make_async_copy(
                    rest[i].at[:, :, lanes], held[i].at[:, :, lanes], arrived.at[2 + 2 * g + i]
                )
                for i in range(2)
            ]
        )
    pieces[0][0].start()
    pieces[0][1].start()
    mats[0].start()
    for piece in pieces[1:]:
        piece[0].start()
        piece[1].start()
    mats[1].start()
    places = partners(slabs, 1)
    outs = views(outs, places, 0, slabs)
    chosen = [(occ_at[start + p], emp_at[start + p]) for p in range(GROUP)]
    for g in range(steps):
        lanes = slice(g * width, (g + 1) * width)
        pieces[g][0].wait()
        pieces[g][1].wait()
        for p in range(GROUP):
            o, e = chosen[p]
            prod[p * planes : (p + 1) * planes, :] = (
                occ[o, :, lanes] * emp[e, :, lanes]
            )
        if g == 0:
            mats[0].wait()
        along = jnp.dot(prod[...], zmat[...], preferred_element_type=F32).astype(BF16)
        for n in range(slabs):
            lines[n, :, g * LANES : (g + 1) * LANES] = along[:, n * LANES : (n + 1) * LANES]
    mats[1].wait()
    for s in range(slabs):
        along = jnp.dot(lines[places[s]], ymat[...], preferred_element_type=F32).astype(BF16)
        first = 0
        for h, wide in enumerate(widths):
            outs[h * slabs + s][...] = along[:, first : first + wide]
            first += wide


def front(start, slabs, widths, occ_at, emp_at, *held):
    occ, _, zmat, ymat = held
    rows = GROUP * occ.shape[1]
    width = zmat.shape[0]
    steps = occ.shape[2] // width
    smem = pl.BlockSpec(memory_space=pltpu.SMEM)
    vmem = pl.BlockSpec(memory_space=pltpu.VMEM)
    out_shape = [o for w in widths for o in shapes(slabs, rows, w, False)]
    outs = pl.pallas_call(
        functools.partial(front_kernel, start, slabs, widths),
        out_shape=out_shape,
        in_specs=[smem] * 2 + [pl.BlockSpec(memory_space=pl.ANY)] * 4,
        out_specs=[vmem] * len(out_shape),
        scratch_shapes=[
            pltpu.VMEM((rows, width), BF16),
            pltpu.VMEM((slabs, rows, ymat.shape[0]), BF16),
        ]
        + [pltpu.VMEM(h.shape, BF16) for h in held]
        + [pltpu.SemaphoreType.DMA((2 + 2 * steps,))],
        compiler_params=pltpu.CompilerParams(vmem_limit_bytes=56 * MIB),
        cost_estimate=COST,
        name="front",
    )(occ_at, emp_at, *held)
    each = len(outs) // len(widths)
    return [outs[h * each : (h + 1) * each] for h in range(len(widths))]


def across_kernel(slabs, blocks, first, grid, part, taken, after, *rest):
    places = partners(slabs, blocks)
    parts = views(rest[:taken], places, 0, slabs)
    xmat, swap = rest[taken : taken + 2]
    outs, whole = views(rest[taken + 2 + after : -1], places, slabs, blocks), rest[-1]
    count = whole.shape[0]
    half = 0 if part is None else places[slabs] // count ^ part
    tall = grid // blocks * count
    rows, wide = parts[0].shape
    planes = rows // GROUP
    channels = grid // slabs
    lane = first + lax.broadcasted_iota(jnp.int32, (tall, wide), 1)
    kx = half * tall + lax.broadcasted_iota(jnp.int32, (tall, wide), 0)
    kx = jnp.where(kx < grid // 2, kx, kx - grid)
    ky = lane // channels
    ky = jnp.where(ky < grid // 4, ky, ky - grid // 2)
    kz = places[0] * (channels // 2) + lane % channels // 2
    squared = (kx * kx + ky * ky + kz * kz).astype(F32)
    quarter = float(grid // 4)
    coulomb = (1.0 / jnp.sqrt(1.0 + squared / (quarter * quarter)))[:, None, :]
    rows_here = pl.ds(half * (8 * tall), 8 * tall)
    left = jnp.concatenate([xmat[places[s], rows_here, :] for s in range(slabs)], axis=1)
    found = []
    for m in range(GROUP // 8):
        right = []
        for s in range(slabs):
            plain = parts[s][m * 8 * planes : (m + 1) * 8 * planes, :]
            right.append(plain)
            turned = [
                jnp.dot(plain[:, c : c + 2 * LANES], swap[...], preferred_element_type=F32)
                for c in range(0, wide, 2 * LANES)
            ]
            right.append(jnp.concatenate(turned, axis=1).astype(BF16))
        right = jnp.concatenate(right, axis=0)
        total = jnp.dot(left, right, preferred_element_type=F32)
        found.append(total.reshape(tall, 8, wide) * coulomb)
    found = jnp.concatenate(found, axis=1).astype(BF16)
    whole[...] = found.reshape(whole.shape)
    for i in range(count):
        at = places[slabs + (part or 0) * count + i]
        outs[i][...] = whole[at - half * count]


def across(slabs, blocks, first, grid, parts, xmat, swap, part, after):
    rows, wide = parts[0].shape[-2:]
    tall = grid // blocks * GROUP
    count = blocks if part is None else blocks // 2
    out_shape = shapes(count, tall, wide, part is None)
    vmem = pl.BlockSpec(memory_space=pltpu.VMEM)
    return pl.pallas_call(
        functools.partial(across_kernel, slabs, blocks, first, grid, part, len(parts), len(after)),
        out_shape=out_shape,
        in_specs=[vmem] * (len(parts) + 2)
        + [pl.BlockSpec(memory_space=pl.ANY)] * len(after),
        out_specs=[vmem] * len(out_shape),
        scratch_shapes=[pltpu.VMEM((count, tall, wide), BF16)],
        compiler_params=pltpu.CompilerParams(vmem_limit_bytes=24 * MIB),
        cost_estimate=COST,
        name="across",
    )(*parts, xmat, swap, *after)


def project_kernel(blocks, slabs, widths, after, held, trial, *rest):
    shares = rest[-1]
    parts, earlier = rest[: -1 - after - held], rest[-1 - after - held : -1 - after]
    places = partners(slabs, blocks)
    parts = views(parts, places, slabs, blocks)
    for ref in earlier:
        shares[:, : ref.shape[1], :] = ref[...]
    below = shares.shape[1] - GROUP
    lanes = sum(widths)
    heights = parts[0].shape[0] // GROUP
    total = jnp.zeros((blocks * GROUP, trial.shape[1]), F32)
    for x in range(heights):
        first = x * lanes
        for h, wide in enumerate(widths):
            left = jnp.concatenate(
                [parts[h * blocks + s][x * GROUP : (x + 1) * GROUP, :] for s in range(blocks)], axis=0
            )
            total += jnp.dot(left, trial[first : first + wide, :], preferred_element_type=F32)
            first += wide
    step = trial.shape[1] // slabs
    for s in range(blocks):
        for n in range(slabs):
            shares[places[slabs + s] * slabs + n, below:, :] = total[
                s * GROUP : (s + 1) * GROUP, n * step : (n + 1) * step
            ].astype(shares.dtype)


def project(blocks, slabs, widths, trial, parts, earlier, after):
    columns, vectors = trial.shape
    pairs = blocks * GROUP
    height = GROUP + sum(e.shape[1] for e in earlier)
    vmem = pl.BlockSpec(memory_space=pltpu.VMEM)
    return pl.pallas_call(
        functools.partial(project_kernel, blocks, slabs, widths, len(after), len(earlier)),
        out_shape=jax.ShapeDtypeStruct((blocks * slabs, height, vectors // slabs), BF16),
        in_specs=[vmem] * (1 + len(parts) + len(earlier))
        + [pl.BlockSpec(memory_space=pl.ANY)] * len(after),
        out_specs=vmem,
        compiler_params=pltpu.CompilerParams(vmem_limit_bytes=24 * MIB),
        cost_estimate=COST,
        name="project",
    )(trial, *parts, *earlier, *after)


def turn_kernel(blocks, slabs, widths, *rest):
    places = partners(slabs, blocks)
    parts, turned = views(rest[:-1], places, slabs, blocks), rest[-1]
    lanes = sum(widths)
    for x in range(parts[0].shape[0] // GROUP):
        first = x * lanes
        for h, wide in enumerate(widths):
            left = [parts[h * blocks + s][x * GROUP : (x + 1) * GROUP, :] for s in range(blocks)]
            turned[first : first + wide, :] = jnp.concatenate(left, axis=0).T
            first += wide


def turn(blocks, slabs, widths, columns, parts):
    vmem = pl.BlockSpec(memory_space=pltpu.VMEM)
    return pl.pallas_call(
        functools.partial(turn_kernel, blocks, slabs, widths),
        out_shape=jax.ShapeDtypeStruct((columns, blocks * GROUP), BF16),
        in_specs=[vmem] * len(parts),
        out_specs=vmem,
        compiler_params=pltpu.CompilerParams(vmem_limit_bytes=16 * MIB),
        cost_estimate=COST,
        name="turn",
    )(*parts)


def respond_kernel(blocks, slabs, groups, freqs, *rest):
    shares, weights, turned = rest[0], rest[1], rest[2 : groups + 2]
    out, weighted = rest[groups + 2 :]
    places = partners(slabs, blocks)
    vectors = out.shape[2]
    step = vectors // slabs

    @pl.when(pl.program_id(0) == 0)
    def _():
        for g in range(groups):
            for s in range(blocks):
                source = places[slabs + s]
                row = (g * blocks + s) * GROUP
                scale = weights[source, g]
                for n in range(slabs):
                    share = shares[source * slabs + n, g * GROUP : (g + 1) * GROUP, :].astype(F32)
                    for w in range(freqs):
                        weighted[w, row : row + GROUP, n * step : (n + 1) * step] = (
                            scale[:, w : w + 1] * share
                        ).astype(BF16)

    left = jnp.concatenate([t[...] for t in turned], axis=1)
    for w in range(freqs):
        out[w] = jnp.dot(left, weighted[w], preferred_element_type=F32).astype(BF16)


def respond(blocks, slabs, shares, weights, turned, vectors):
    groups = len(turned)
    columns, pairs = turned[0].shape
    freqs = weights.shape[-1]
    height = min(columns, 512)
    vmem = pl.BlockSpec(memory_space=pltpu.VMEM)
    return pl.pallas_call(
        functools.partial(respond_kernel, blocks, slabs, groups, freqs),
        grid=(columns // height,),
        out_shape=jax.ShapeDtypeStruct((freqs, columns, vectors), BF16),
        in_specs=[vmem] * 2
        + [pl.BlockSpec((height, pairs), lambda i: (i, 0))] * groups,
        out_specs=pl.BlockSpec((freqs, height, vectors), lambda i: (0, i, 0)),
        scratch_shapes=[pltpu.VMEM((freqs, groups * pairs, vectors), BF16)],
        compiler_params=pltpu.CompilerParams(vmem_limit_bytes=16 * MIB + 4 * freqs * vectors * (groups * pairs + height)),
        cost_estimate=COST,
        name="respond",
    )(shares, weights, *turned)


def exchange(blocks, axis):
    if len(blocks) == 1:
        return [lax.all_to_all(blocks[0], axis, 0, 0, tiled=True)]
    return [blocks[0]] + [
        lax.ppermute(blocks[s], axis, [(i, i ^ s) for i in range(len(blocks))])
        for s in range(1, len(blocks))
    ]


def sum_shares(shares):
    both = ("wide", "narrow")
    count = shares.shape[0]
    taken = lax.all_to_all(shares, both, 0, 0, tiled=True)
    total = jnp.sum(taken.astype(F32), axis=0, keepdims=True).astype(BF16)
    spread = jnp.broadcast_to(total, (count,) + total.shape[1:])
    return lax.all_to_all(spread, both, 0, 0, tiled=True)


def shards(occupied, empty, pair_occ, pair_emp, pair_level, denominators, trial):
    slabs = lax.axis_size("narrow")
    blocks = lax.axis_size("wide")
    grid = occupied.shape[1] * slabs
    zmat, ymat, xmat, swap = (jnp.asarray(t) for t in tables(grid, slabs))
    lanes = ymat.shape[1]
    groups = pair_occ.shape[0] // GROUP
    vectors = trial.shape[1]
    levels = jnp.arange(denominators.shape[0], dtype=jnp.int32)
    onehot = (pair_level[:, None] == levels[None, :]).astype(F32)
    weights = jnp.dot(onehot, denominators, precision=lax.Precision.HIGHEST)
    weights = weights.reshape(blocks, groups, GROUP, -1)

    sent, waves = {}, {}
    for g in range(groups):
        cut = SPLITS[g % len(SPLITS)]
        widths = tuple(lanes * c // sum(cut) for c in cut)
        sent[g] = widths, front(
            g * GROUP, slabs, widths, pair_occ, pair_emp, occupied, empty, zmat, ymat
        )
    for g in range(groups):
        first, waves[g] = 0, []
        after = [blocked[0] for blocked in sent[g + 1][1]] if g + 1 < groups else []
        for wide, blocked in zip(*sent[g]):
            got = exchange(blocked, "narrow")
            if blocks > PERMUTE_MOST:
                stack = across(slabs, blocks, first, grid, got, xmat, swap, None, after)
                waves[g].append(stack)
            else:
                far = across(slabs, blocks, first, grid, got, xmat, swap, 1, after)
                near = across(slabs, blocks, first, grid, got, xmat, swap, 0, far[:1])
                waves[g].append(list(near) + list(far))
            first += wide
    shares, turned = [], []
    for g in range(groups):
        parts = [piece for blocked in waves[g] for piece in exchange(blocked, "wide")]
        after = [blocked[0] for blocked in waves.get(g + 1, [])]
        widths = sent[g][0]
        shares = [project(blocks, slabs, widths, trial, parts, shares, after)]
        turned.append(turn(blocks, slabs, widths, trial.shape[0], parts))
    shares = sum_shares(shares[0])
    return respond(
        blocks,
        slabs,
        shares,
        weights,
        turned,
        vectors,
    )


def solution(mesh):
    placed = (
        P("wide", "narrow", None),
        P("wide", "narrow", None),
        P("wide"),
        P("wide"),
        P(),
        P(),
        P(("wide", "narrow"), None),
    )
    return jax.shard_map(
        shards,
        mesh=mesh,
        in_specs=placed,
        out_specs=P(None, ("wide", "narrow"), None),
        check_vma=False,
    )
```
